32 devices in a mesh: rows: 2 (over x), bx: 4 (over y, core), by: 4 (over z).
Axes of the slice: x: 2, y: 2, z: 4, core: 2. Of those that a mesh axis runs over, the one named last changes fastest.
Arguments:
- pair_mult: bfloat16 [131072, 256], P(('rows', 'bx', 'by')), may hold values from -1.5 to 1.5
- pair_dens: float32 [131072], P(('rows', 'bx', 'by')), may hold values from -3 to 3
- pair_live: int32 [131072], P(('rows', 'bx', 'by')), may hold values 0 or 1
- pair_box: int32 [131072], P(('rows', 'bx', 'by')), may hold values from 0 to 767
- inter_mask: int32 [16, 32, 32, 98], P('rows', 'bx', 'by'), may hold values 0 or 1
- row_scale: float32 [98, 256], replicated, may hold values from 0.3 to 1.5
- col_scale: float32 [98, 256], replicated, may hold values from 0.3 to 1.5
- base: bfloat16 [256, 256], replicated, may hold values from -0.0390625 to 0.0390625
- lattice: float32 [256, 256], replicated, may hold values from -0.0029296875 to 0.0029296875
Outputs:
- box_locals: bfloat16 [16, 32, 32, 256], P('rows', 'bx', 'by')
- pair_j: float32 [131072], P(('rows', 'bx', 'by'))
The draws below stay inside these ranges and needn't reach their ends.
Inputs may be any that keep to these rules, and one draw needn't show every extreme that they name: `pair_box`: numbers a box of the pair's own x, y slab as (l * 8 + x) * 8 + y with l in 0..11, x in 0..7, y in 0..7, where level l is the box z = (rows index of the device * 8 + l - 2) mod 16.
All inputs are finite; a program needn't handle non-finite values. No bound on the sum of `pair_live` or of `inter_mask` on one device may be relied on, other than what follows from the above.
Results may differ from the reference program's by a relative error of at most 0.007.
Values may be sent and summed in bfloat16 or wider, within the bound.
A program may use at most 128 MiB of HBM per device.

```python
import math
import jax
import jax.numpy as jnp
import numpy as np
from jax import lax

NC = 256
OFFS = 98
BXL = 8
BYL = 8
BZL = 8
PAIR_DEV = 4096
NBX = 32
NBY = 32
NBZ = 16
NEAR = 768
PAIRS = 131072
N_BX = 4
N_BY = 4
DEVICES = 32


def place_ends(result, stream_key, smallest, high):
    place = [jax.random.randint(jax.random.fold_in(stream_key, axis), (), 0, length) for axis, length in enumerate(result.shape)]
    widest = result.shape.index(max(result.shape))
    beside = place[:widest] + [(place[widest] + 1) % result.shape[widest]] + place[widest + 1:]
    return result.at[tuple(place)].set(smallest).at[tuple(beside)].set(high)


def shard_levels(rng, extent, shards, least, top_value):
    loudness = 1.0
    for axis_at, parts in shards:
        steps = jax.random.uniform(jax.random.fold_in(jax.random.fold_in(rng, 6), axis_at), (parts,), jnp.float32, least / len(shards), top_value / len(shards))
        loudness = loudness * jnp.repeat(jnp.exp(steps), extent[axis_at] // parts).reshape((-1,) + (1,) * (len(extent) - 1 - axis_at))
    return loudness


def cumulative_ranks(count, slope):
    weights = [(1 << 20) // math.isqrt(standing ** slope) + 1 for standing in range(1, count + 1)]
    deviation = 1 + sum(weights) // (1 << 30)
    return np.cumsum(np.array([max(1, weight // deviation) for weight in weights]))


def ranked(rng, dims, number_of, slope):
    table = cumulative_ranks(number_of, slope)
    lot = jax.random.randint(jax.random.fold_in(rng, 1), dims, 0, int(table[number_of - 1]))
    standing = jnp.searchsorted(jnp.asarray(table, jnp.int32), lot, side="right")
    return jax.random.permutation(jax.random.fold_in(rng, 2), number_of)[standing].astype(jnp.int32)


def centred(own_key, extent, width, reach, shards=(), held_as=jnp.bfloat16):
    values = jax.random.normal(own_key, extent, jnp.float32) * width
    if len(shards) > 0:
        values = shard_levels(own_key, extent, shards, -0.22, 0.18) * values
    return jnp.clip(values, min=-reach, max=reach).astype(held_as)


def setup_inputs(seed: int = 0) -> dict:
    seeds = jax.random.split(jax.random.key(seed), 10)
    return {
        "pair_mult": centred(seeds[0], (PAIRS, NC), 0.25, 1.5, ((0, 32),)),
        "pair_dens": centred(seeds[1], (PAIRS,), 0.5, 3.0, ((0, 32),), jnp.float32),
        "pair_live": place_ends((jax.random.randint(seeds[2], (PAIRS,), 0, 4) < 3).astype(jnp.int32), jax.random.fold_in(seeds[2], 1), 0, 1),
        "pair_box": place_ends(ranked(seeds[3], (PAIRS,), NEAR, 2), jax.random.fold_in(seeds[3], 3), 0, NEAR - 1).astype(jnp.int32),
        "inter_mask": place_ends((jax.random.randint(seeds[4], (NBZ, NBX, NBY, OFFS), 0, 4) < 3).astype(jnp.int32), jax.random.fold_in(seeds[4], 1), 0, 1),
        "row_scale": jnp.clip(jnp.exp(jax.random.uniform(seeds[5], (OFFS, NC), jnp.float32, math.log(0.3), math.log(1.5))), 0.3, 1.5),
        "col_scale": jnp.clip(jnp.exp(jax.random.uniform(seeds[6], (OFFS, NC), jnp.float32, math.log(0.3), math.log(1.5))), 0.3, 1.5),
        "base": centred(seeds[7], (NC, NC), (NC * OFFS) ** -0.5, 0.0390625),
        "lattice": centred(seeds[8], (NC, NC), (NC * NBX * NBY * NBZ) ** -0.5, 0.0029296875, (), jnp.float32),
    }


def offset_table():
    listed = []
    for shift_z in range(-2, 3):
        for shift_x in range(-2, 3):
            for shift_y in range(-2, 3):
                if max(abs(shift_z), abs(shift_x), abs(shift_y)) == 2:
                    listed.append((shift_z, shift_x, shift_y))
    return listed


def reference(pair_mult, pair_dens, pair_live, pair_box, inter_mask, row_scale, col_scale, base, lattice):
    weighted = ((pair_dens * pair_live.astype(jnp.float32))[:, None] * pair_mult.astype(jnp.float32)).astype(jnp.bfloat16)
    device = jnp.arange(PAIRS, dtype=jnp.int32) // PAIR_DEV
    row_index = device // (N_BX * N_BY)
    slab_x = (device // N_BY) % N_BX
    slab_y = device % N_BY
    level = (row_index * BZL + pair_box // (BXL * BYL) - 2) % NBZ
    xpos = slab_x * BXL + (pair_box // BYL) % BXL
    ypos = slab_y * BYL + pair_box % BYL
    box_id = ((level * NBX + xpos) * NBY + ypos).astype(jnp.int32)
    weighted_wide = weighted.astype(jnp.float32)
    moments = jax.ops.segment_sum(weighted_wide, box_id, NBZ * NBX * NBY)
    cell = jnp.sum(weighted_wide, 0)
    stored = moments.reshape(NBZ, NBX, NBY, NC)
    far = jnp.zeros((NBZ, NBX, NBY, NC), jnp.float32)
    for entry, shifts in enumerate(offset_table()):
        source = jnp.roll(stored, (-shifts[0], -shifts[1], -shifts[2]), (0, 1, 2))
        gate_values = inter_mask[..., entry].astype(jnp.float32)[..., None]
        scaled = (source * gate_values * row_scale[entry]).astype(jnp.bfloat16)
        product = jnp.dot(scaled.reshape(-1, NC), base, preferred_element_type=jnp.float32)
        far = far + product.reshape(NBZ, NBX, NBY, NC) * col_scale[entry]
    lattice_term = jnp.dot(cell, lattice, precision=lax.Precision.HIGHEST)
    box_locals = (far + lattice_term).astype(jnp.bfloat16)
    flat_locals = box_locals.reshape(-1, NC)

    def pair_block(packed):
        mult_block, id_block = packed
        picked = flat_locals[id_block].astype(jnp.float32)
        return jnp.sum(mult_block.astype(jnp.float32) * picked, -1)

    pair_j = lax.map(pair_block, (pair_mult.reshape(DEVICES, PAIR_DEV, NC), box_id.reshape(DEVICES, PAIR_DEV)))
    return box_locals, pair_j.reshape(PAIRS)
```

```python
import functools

import jax
import jax.numpy as jnp
from jax import lax
from jax.experimental import pallas as pl
from jax.experimental.pallas import tpu as pltpu
from jax.sharding import PartitionSpec as P

PAIR_CHUNK = 512
VMEM = pl.BlockSpec(memory_space=pltpu.VMEM)


def offset_table():
    listed = []
    for shift_z in range(-2, 3):
        for shift_x in range(-2, 3):
            for shift_y in range(-2, 3):
                if max(abs(shift_z), abs(shift_x), abs(shift_y)) == 2:
                    listed.append((shift_z, shift_x, shift_y))
    return listed


def moments_kernel(mult_ref, dens_ref, live_ref, box_ref, near_ref, cell_ref):
    near = near_ref.shape[0]
    labels = lax.broadcasted_iota(jnp.int32, (near, PAIR_CHUNK), 0)
    near_ref[...] = jnp.zeros_like(near_ref)

    def step(index, carry):
        at = pl.ds(pl.multiple_of(index * PAIR_CHUNK, PAIR_CHUNK), PAIR_CHUNK)
        weight = dens_ref[:, at] * live_ref[:, at].astype(jnp.float32)
        selector = jnp.where(labels == box_ref[:, at], weight, 0.0).astype(jnp.bfloat16)
        near_ref[...] += jnp.dot(selector, mult_ref[at, :], preferred_element_type=jnp.float32)
        return carry

    lax.fori_loop(0, mult_ref.shape[0] // PAIR_CHUNK, step, 0)
    cell_ref[...] = jnp.sum(near_ref[...], 0, keepdims=True)


def pairs_kernel(locals_ref, mult_ref, box_ref, out_ref):
    near = locals_ref.shape[0]
    labels = lax.broadcasted_iota(jnp.int32, (near, PAIR_CHUNK), 0)

    def step(index, carry):
        at = pl.ds(pl.multiple_of(index * PAIR_CHUNK, PAIR_CHUNK), PAIR_CHUNK)
        values = lax.dot_general(
            locals_ref[...],
            mult_ref[at, :],
            (((1,), (1,)), ((), ())),
            preferred_element_type=jnp.float32,
        )
        hits = jnp.where(labels == box_ref[:, at], values, 0.0)
        out_ref[:, at] = jnp.sum(hits, 0, keepdims=True)
        return carry

    lax.fori_loop(0, mult_ref.shape[0] // PAIR_CHUNK, step, 0)


def expand_operators(rows_ref, cols_ref, base_ref, wide_ref):
    offsets, comps, outs = wide_ref.shape

    def step(index, carry):
        at = pl.ds(pl.multiple_of(index * 16, 16), 16)
        core = base_ref[at, :].astype(jnp.float32)
        rows = rows_ref[at, :]
        for entry in range(offsets):
            scaled = core * rows[:, entry : entry + 1] * cols_ref[entry : entry + 1, :]
            wide_ref[entry, at, :] = scaled.astype(jnp.bfloat16)
        return carry

    lax.fori_loop(0, comps // 16, step, 0)


def expand_masks(mask_ref, wide_ref):
    offsets, boxes, lanes = wide_ref.shape

    def step(index, carry):
        at = pl.ds(pl.multiple_of(index * 32, 32), 32)
        gates = mask_ref[at, :].astype(jnp.float32)
        for entry in range(offsets):
            wide = jnp.broadcast_to(gates[:, entry : entry + 1], (32, lanes))
            wide_ref[entry, at, :] = wide.astype(jnp.bfloat16)
        return carry

    lax.fori_loop(0, boxes // 32, step, 0)


def shifted_copies(padded_ref, shifted_ref):
    depth = padded_ref.shape[0]
    size_y = padded_ref.shape[2] - 4
    spread_x = padded_ref.shape[1]
    comps = padded_ref.shape[3]

    def step(level, carry):
        for move in range(5):
            part = padded_ref[level, :, move : move + size_y, :].astype(jnp.bfloat16)
            shifted_ref[move, 0, level] = part.reshape(spread_x * size_y, comps)
            part = padded_ref[level, 1 : spread_x - 1, move : move + size_y, :].astype(jnp.bfloat16)
            shifted_ref[move, 1, level, : (spread_x - 2) * size_y] = part.reshape(
                (spread_x - 2) * size_y, comps
            )
        return carry

    lax.fori_loop(0, depth, step, 0)


def far_field(shifted_ref, gates_ref, wide_ref, total_ref, left_ref, sizes):
    size_z, size_x, size_y = sizes
    rows = size_x * size_y
    boxes = size_z * rows
    comps = wide_ref.shape[1]

    def group(shift_z, shift_x, first, moves):
        even = (shift_x + 2) % 2
        start = pl.multiple_of(((shift_x + 2) // 2) * 2 * size_y, 2 * size_y)
        for place, move in enumerate(moves):
            source = shifted_ref[move + 2, even, pl.ds(shift_z + 2, size_z), pl.ds(start, rows), :]
            source = source.reshape(boxes, comps)
            gate = gates_ref[first + place]
            for half in range(comps // 128):
                lanes = slice(half * 128, half * 128 + 128)
                left_ref[:, place * comps + half * 128 : place * comps + half * 128 + 128] = (
                    source[:, lanes] * gate
                )
        count = len(moves)
        operator = wide_ref[pl.ds(first, count)].reshape(count * comps, comps)
        total_ref[...] += jnp.dot(
            left_ref[:, : count * comps], operator, preferred_element_type=jnp.float32
        )

    def outer(index, carry):
        side, spot = index // 5, index % 5
        group(side * 4 - 2, spot - 2, side * 73 + spot * 5, (-2, -1, 0, 1, 2))
        return carry

    def edge(index, carry):
        level, side = index // 2, index % 2
        group(level - 1, side * 4 - 2, 25 + level * 16 + side * 11, (-2, -1, 0, 1, 2))
        return carry

    def inner(index, carry):
        level, spot = index // 3, index % 3
        group(level - 1, spot - 1, 30 + level * 16 + spot * 2, (-2, 2))
        return carry

    lax.fori_loop(0, 10, outer, 0)
    lax.fori_loop(0, 6, edge, 0)
    lax.fori_loop(0, 9, inner, 0)


def field_kernel(
    sizes, padded_ref, mask_ref, rows_ref, cols_ref, base_ref, term_ref, out_ref,
    gates_ref, wide_ref, shifted_ref, left_ref, total_ref,
):
    expand_operators(rows_ref, cols_ref, base_ref, wide_ref)
    expand_masks(mask_ref, gates_ref)
    shifted_copies(padded_ref, shifted_ref)
    total_ref[...] = jnp.broadcast_to(term_ref[...], total_ref.shape)
    far_field(shifted_ref, gates_ref, wide_ref, total_ref, left_ref, sizes)
    out_ref[...] = total_ref[...].astype(jnp.bfloat16)


def ring(axis):
    count = lax.axis_size(axis)
    up = [(i, (i + 1) % count) for i in range(count)]
    return up, [(j, i) for i, j in up]


def padded_2(x, axis, dim):
    up, down = ring(axis)
    length = x.shape[dim]
    before = lax.ppermute(lax.slice_in_dim(x, length - 2, length, axis=dim), axis, up)
    after = lax.ppermute(lax.slice_in_dim(x, 0, 2, axis=dim), axis, down)
    return jnp.concatenate([before, x, after], axis=dim)


def per_device(
    pair_mult, pair_dens, pair_live, pair_box, inter_mask, row_scale, col_scale, base, lattice
):
    pairs, comps = pair_mult.shape
    depth, width_x, width_y, offsets = inter_mask.shape
    boxes = depth * width_x * width_y
    near = (depth + 4) * width_x * width_y
    box_row = pair_box.reshape(1, pairs)
    params = pltpu.CompilerParams(vmem_limit_bytes=56 * 1024 * 1024)
    partial, cell_part = pl.pallas_call(
        moments_kernel,
        out_shape=(
            jax.ShapeDtypeStruct((near, comps), jnp.float32),
            jax.ShapeDtypeStruct((1, comps), jnp.float32),
        ),
        in_specs=[VMEM] * 4,
        out_specs=(VMEM, VMEM),
        compiler_params=params,
    )(pair_mult, pair_dens.reshape(1, pairs), pair_live.reshape(1, pairs), box_row)
    cell = lax.psum(cell_part, ("rows", "bx", "by"))
    term = jnp.dot(cell, lattice, precision=lax.Precision.HIGHEST)

    partial = partial.reshape(depth + 4, width_x, width_y, comps)
    up, down = ring("rows")
    low = lax.ppermute(partial[depth:].astype(jnp.bfloat16), "rows", up)
    high = lax.ppermute(partial[:4].astype(jnp.bfloat16), "rows", down)
    full = jnp.concatenate(
        [
            partial[:4] + low.astype(jnp.float32),
            partial[4:depth],
            partial[depth:] + high.astype(jnp.float32),
        ],
        axis=0,
    ).astype(jnp.bfloat16)
    padded = padded_2(padded_2(full, "bx", 1), "by", 2).astype(jnp.float32)

    box_locals = pl.pallas_call(
        functools.partial(field_kernel, (depth, width_x, width_y)),
        out_shape=jax.ShapeDtypeStruct((boxes, comps), jnp.bfloat16),
        in_specs=[VMEM] * 6,
        out_specs=VMEM,
        scratch_shapes=[
            pltpu.VMEM((offsets, boxes, 128), jnp.bfloat16),
            pltpu.VMEM((offsets, comps, comps), jnp.bfloat16),
            pltpu.VMEM((5, 2, depth + 4, (width_x + 4) * width_y, comps), jnp.bfloat16),
            pltpu.VMEM((boxes, 5 * comps), jnp.bfloat16),
            pltpu.VMEM((boxes, comps), jnp.float32),
        ],
        compiler_params=params,
    )(padded, inter_mask.reshape(boxes, offsets), row_scale.T, col_scale, base, term)

    box_locals = box_locals.reshape(depth, width_x, width_y, comps)
    near_locals = padded_2(box_locals, "rows", 0).reshape(near, comps)
    pair_j = pl.pallas_call(
        pairs_kernel,
        out_shape=jax.ShapeDtypeStruct((1, pairs), jnp.float32),
        in_specs=[VMEM] * 3,
        out_specs=VMEM,
        compiler_params=params,
    )(near_locals, pair_mult, box_row)
    return (box_locals, pair_j.reshape(pairs))


def solution(mesh):
    return jax.shard_map(
        per_device,
        mesh=mesh,
        in_specs=(
            P(("rows", "bx", "by"), None),
            P(("rows", "bx", "by")),
            P(("rows", "bx", "by")),
            P(("rows", "bx", "by")),
            P("rows", "bx", "by", None),
            P(),
            P(),
            P(),
            P(),
        ),
        out_specs=(P("rows", "bx", "by", None), P(("rows", "bx", "by"))),
        check_vma=False,
    )
```

```python
import functools

import jax
import jax.numpy as jnp
from jax import lax
from jax.experimental import pallas as pl
from jax.experimental.pallas import tpu as pltpu
from jax.sharding import PartitionSpec as P

PAIR_CHUNK = 512
VMEM = pl.BlockSpec(memory_space=pltpu.VMEM)


def offset_table():
    listed = []
    for shift_z in range(-2, 3):
        for shift_x in range(-2, 3):
            for shift_y in range(-2, 3):
                if max(abs(shift_z), abs(shift_x), abs(shift_y)) == 2:
                    listed.append((shift_z, shift_x, shift_y))
    return listed


def add_moments(mult_ref, dens_ref, live_ref, box_ref, near_ref):
    near = near_ref.shape[0]
    labels = lax.broadcasted_iota(jnp.int32, (near, PAIR_CHUNK), 0)
    near_ref[...] = jnp.zeros_like(near_ref)

    def step(index, carry):
        at = pl.ds(pl.multiple_of(index * PAIR_CHUNK, PAIR_CHUNK), PAIR_CHUNK)
        weight = dens_ref[:, at] * live_ref[:, at].astype(jnp.float32)
        selector = jnp.where(labels == box_ref[:, at], weight, 0.0).astype(jnp.bfloat16)
        near_ref[...] += jnp.dot(selector, mult_ref[at, :], preferred_element_type=jnp.float32)
        return carry

    lax.fori_loop(0, mult_ref.shape[0] // PAIR_CHUNK, step, 0)


def add_pairs(locals_ref, first, mult_ref, box_ref, pairs_ref, fresh):
    count = locals_ref.shape[0]
    labels = lax.broadcasted_iota(jnp.int32, (count, PAIR_CHUNK), 0) + first

    def step(index, carry):
        at = pl.ds(pl.multiple_of(index * PAIR_CHUNK, PAIR_CHUNK), PAIR_CHUNK)
        values = lax.dot_general(
            locals_ref[...],
            mult_ref[at, :],
            (((1,), (1,)), ((), ())),
            preferred_element_type=jnp.float32,
        )
        hits = jnp.where(labels == box_ref[:, at], values, 0.0)
        found = jnp.sum(hits, 0, keepdims=True)
        pairs_ref[:, at] = found if fresh else pairs_ref[:, at] + found
        return carry

    lax.fori_loop(0, mult_ref.shape[0] // PAIR_CHUNK, step, 0)


def neighbour(axis, move):
    count = lax.axis_size(axis)
    return {axis: lax.rem(lax.axis_index(axis) + (move + count), count)}


def send(source, target, sems, index, device):
    copy = pltpu.make_async_remote_copy(
        src_ref=source,
        dst_ref=target,
        send_sem=sems.at[0, index],
        recv_sem=sems.at[1, index],
        device_id=device,
        device_id_type=pl.DeviceIdType.MESH,
    )
    copy.start()
    return copy


def share_cells(axis, own_ref, slots_ref, sems):
    return [
        send(own_ref, slots_ref.at[move - 1], sems, move - 1, neighbour(axis, move))
        for move in range(1, lax.axis_size(axis))
    ]


def collect_cells(copies, own_ref, slots_ref):
    value = own_ref[...]
    for place, copy in enumerate(copies):
        copy.wait_recv()
        value = value + slots_ref[place]
    return value


def fused_kernel(
    sizes, mult_ref, dens_ref, live_ref, box_ref, mask_ref, rows_ref, cols_ref, base_ref, lattice_ref,
    out_ref, pairs_ref,
    near_ref, zsend_ref, zrecv_ref, full_ref, padded_ref, pack_ref, ysend_ref, yrecv_ref, lrecv_ref,
    cells_ref, cells_r, cells_x, cells_y, gates_ref, wide_ref, shifted_ref, left_ref, total_ref,
    zsem, xsem, ysem, lsem, crsem, cxsem, cysem,
):
    size_z, size_x, size_y = sizes
    plane = size_x * size_y
    near_z, near_x = size_z + 4, size_x + 4
    comps = near_ref.shape[1]
    axes = ("rows", "bx", "by")
    barrier = pltpu.get_barrier_semaphore()
    peers = 0
    for axis in axes:
        for move in range(1, lax.axis_size(axis)):
            pl.semaphore_signal(
                barrier, inc=1, device_id=neighbour(axis, move), device_id_type=pl.DeviceIdType.MESH
            )
            peers += 1

    add_moments(mult_ref, dens_ref, live_ref, box_ref, near_ref)
    zsend_ref[0] = near_ref[: 4 * plane].astype(jnp.bfloat16)
    zsend_ref[1] = near_ref[size_z * plane :].astype(jnp.bfloat16)
    pl.semaphore_wait(barrier, peers)
    waits = [
        send(zsend_ref.at[0], zrecv_ref.at[1], zsem, 0, neighbour("rows", -1)),
        send(zsend_ref.at[1], zrecv_ref.at[0], zsem, 1, neighbour("rows", 1)),
    ]
    zcopies = list(waits)
    cells_ref[0] = jnp.broadcast_to(jnp.sum(near_ref[...], 0, keepdims=True), (8, comps))
    rcopies = share_cells("rows", cells_ref.at[0], cells_r, crsem)
    waits += rcopies

    expand_operators(rows_ref, cols_ref, base_ref, wide_ref)

    for copy in zcopies:
        copy.wait_recv()
    near_ref[: 4 * plane] += zrecv_ref[0].astype(jnp.float32)
    near_ref[size_z * plane :] += zrecv_ref[1].astype(jnp.float32)
    own = pl.ds(2 * size_y, plane)
    for level in range(near_z):
        full_ref[level, own, :] = near_ref[level * plane : (level + 1) * plane].astype(jnp.bfloat16)
    edge = 2 * size_y
    xcopies = [
        send(
            full_ref.at[:, pl.ds(edge, edge), :], full_ref.at[:, pl.ds(edge + plane, edge), :],
            xsem, 0, neighbour("bx", -1),
        ),
        send(
            full_ref.at[:, pl.ds(plane, edge), :], full_ref.at[:, pl.ds(0, edge), :],
            xsem, 1, neighbour("bx", 1),
        ),
    ]
    waits += xcopies
    cells_ref[1] = collect_cells(rcopies, cells_ref.at[0], cells_r)
    bcopies = share_cells("bx", cells_ref.at[1], cells_x, cxsem)
    waits += bcopies

    expand_masks(mask_ref, gates_ref)

    for copy in xcopies:
        copy.wait_recv()

    def pack(level, carry):
        values = full_ref[level].astype(jnp.float32).reshape(near_x, size_y, comps)
        padded_ref[level, :, 2 : 2 + size_y, :] = values
        for x in range(near_x):
            pack_ref[0, level, 2 * x : 2 * x + 2, :] = values[x, :2, :]
            pack_ref[1, level, 2 * x : 2 * x + 2, :] = values[x, size_y - 2 :, :]
        return carry

    lax.fori_loop(0, near_z, pack, 0)
    ysend_ref[...] = pack_ref[...].reshape(ysend_ref.shape).astype(jnp.bfloat16)
    ycopies = [
        send(ysend_ref.at[0], yrecv_ref.at[1], ysem, 0, neighbour("by", -1)),
        send(ysend_ref.at[1], yrecv_ref.at[0], ysem, 1, neighbour("by", 1)),
    ]
    waits += ycopies
    cells_ref[2] = collect_cells(bcopies, cells_ref.at[1], cells_x)
    ccopies = share_cells("by", cells_ref.at[2], cells_y, cysem)
    waits += ccopies
    for copy in ycopies:
        copy.wait_recv()
    pack_ref[...] = yrecv_ref[...].astype(jnp.float32).reshape(pack_ref.shape)

    def unpack(level, carry):
        for x in range(near_x):
            padded_ref[level, x, :2, :] = pack_ref[0, level, 2 * x : 2 * x + 2, :]
            padded_ref[level, x, 2 + size_y :, :] = pack_ref[1, level, 2 * x : 2 * x + 2, :]
        return carry

    lax.fori_loop(0, near_z, unpack, 0)
    shifted_copies(padded_ref, shifted_ref)

    cell = collect_cells(ccopies, cells_ref.at[2], cells_y)
    term = jnp.dot(
        cell, lattice_ref[...], precision=lax.Precision.HIGHEST, preferred_element_type=jnp.float32
    )
    total_ref[...] = jnp.broadcast_to(term[:1], total_ref.shape)
    far_field(shifted_ref, gates_ref, wide_ref, total_ref, left_ref, sizes)
    out_ref[...] = total_ref[...].astype(jnp.bfloat16)
    boxes = size_z * plane
    lcopies = [
        send(out_ref.at[pl.ds(0, 2 * plane)], lrecv_ref.at[1], lsem, 0, neighbour("rows", -1)),
        send(out_ref.at[pl.ds(boxes - 2 * plane, 2 * plane)], lrecv_ref.at[0], lsem, 1, neighbour("rows", 1)),
    ]
    waits += lcopies
    add_pairs(out_ref, 2 * plane, mult_ref, box_ref, pairs_ref, True)
    for copy in lcopies:
        copy.wait_recv()
    add_pairs(lrecv_ref.at[0], 0, mult_ref, box_ref, pairs_ref, False)
    add_pairs(lrecv_ref.at[1], boxes + 2 * plane, mult_ref, box_ref, pairs_ref, False)
    for copy in waits:
        copy.wait_send()


def per_device(
    pair_mult, pair_dens, pair_live, pair_box, inter_mask, row_scale, col_scale, base, lattice
):
    pairs, comps = pair_mult.shape
    depth, width_x, width_y, offsets = inter_mask.shape
    plane = width_x * width_y
    boxes = depth * plane
    near = boxes + 4 * plane
    edge_rows = (depth + 4) * (width_x + 4) * 2
    counts = [lax.axis_size(axis) - 1 for axis in ("rows", "bx", "by")]
    b16, f32 = jnp.bfloat16, jnp.float32
    box_locals, pair_j = pl.pallas_call(
        functools.partial(fused_kernel, (depth, width_x, width_y)),
        out_shape=(
            jax.ShapeDtypeStruct((boxes, comps), b16),
            jax.ShapeDtypeStruct((1, pairs), f32),
        ),
        in_specs=[VMEM] * 9,
        out_specs=(VMEM, VMEM),
        scratch_shapes=[
            pltpu.VMEM((near, comps), f32),
            pltpu.VMEM((2, 4 * plane, comps), b16),
            pltpu.VMEM((2, 4 * plane, comps), b16),
            pltpu.VMEM((depth + 4, (width_x + 4) * width_y, comps), b16),
            pltpu.VMEM((depth + 4, width_x + 4, width_y + 4, comps), f32),
            pltpu.VMEM((2, depth + 4, 2 * (width_x + 4), comps), f32),
            pltpu.VMEM((2, edge_rows, comps), b16),
            pltpu.VMEM((2, edge_rows, comps), b16),
            pltpu.VMEM((2, 2 * plane, comps), b16),
            pltpu.VMEM((3, 8, comps), f32),
        ]
        + [pltpu.VMEM((count, 8, comps), f32) for count in counts]
        + [
            pltpu.VMEM((offsets, boxes, 128), b16),
            pltpu.VMEM((offsets, comps, comps), b16),
            pltpu.VMEM((5, 2, depth + 4, (width_x + 4) * width_y, comps), b16),
            pltpu.VMEM((boxes, 5 * comps), b16),
            pltpu.VMEM((boxes, comps), f32),
        ]
        + [pltpu.SemaphoreType.DMA((2, 2))] * 4
        + [pltpu.SemaphoreType.DMA((2, count)) for count in counts],
        compiler_params=pltpu.CompilerParams(
            vmem_limit_bytes=56 * 1024 * 1024, collective_id=0, has_side_effects=True
        ),
    )(
        pair_mult, pair_dens.reshape(1, pairs), pair_live.reshape(1, pairs), pair_box.reshape(1, pairs),
        inter_mask.reshape(boxes, offsets), row_scale.T, col_scale, base, lattice,
    )
    return (box_locals.reshape(depth, width_x, width_y, comps), pair_j.reshape(pairs))


def expand_operators(rows_ref, cols_ref, base_ref, wide_ref):
    offsets, comps, outs = wide_ref.shape

    def step(index, carry):
        at = pl.ds(pl.multiple_of(index * 16, 16), 16)
        core = base_ref[at, :].astype(jnp.float32)
        rows = rows_ref[at, :]
        for entry in range(offsets):
            scaled = core * rows[:, entry : entry + 1] * cols_ref[entry : entry + 1, :]
            wide_ref[entry, at, :] = scaled.astype(jnp.bfloat16)
        return carry

    lax.fori_loop(0, comps // 16, step, 0)


def expand_masks(mask_ref, wide_ref):
    offsets, boxes, lanes = wide_ref.shape

    def step(index, carry):
        at = pl.ds(pl.multiple_of(index * 32, 32), 32)
        gates = mask_ref[at, :].astype(jnp.float32)
        for entry in range(offsets):
            wide = jnp.broadcast_to(gates[:, entry : entry + 1], (32, lanes))
            wide_ref[entry, at, :] = wide.astype(jnp.bfloat16)
        return carry

    lax.fori_loop(0, boxes // 32, step, 0)


def shifted_copies(padded_ref, shifted_ref):
    depth = padded_ref.shape[0]
    size_y = padded_ref.shape[2] - 4
    spread_x = padded_ref.shape[1]
    comps = padded_ref.shape[3]

    def step(level, carry):
        for move in range(5):
            part = padded_ref[level, :, move : move + size_y, :].astype(jnp.bfloat16)
            shifted_ref[move, 0, level] = part.reshape(spread_x * size_y, comps)
            part = padded_ref[level, 1 : spread_x - 1, move : move + size_y, :].astype(jnp.bfloat16)
            shifted_ref[move, 1, level, : (spread_x - 2) * size_y] = part.reshape(
                (spread_x - 2) * size_y, comps
            )
        return carry

    lax.fori_loop(0, depth, step, 0)


def far_field(shifted_ref, gates_ref, wide_ref, total_ref, left_ref, sizes):
    size_z, size_x, size_y = sizes
    rows = size_x * size_y
    boxes = size_z * rows
    comps = wide_ref.shape[1]

    def group(shift_z, shift_x, first, moves):
        even = (shift_x + 2) % 2
        start = pl.multiple_of(((shift_x + 2) // 2) * 2 * size_y, 2 * size_y)
        for place, move in enumerate(moves):
            source = shifted_ref[move + 2, even, pl.ds(shift_z + 2, size_z), pl.ds(start, rows), :]
            source = source.reshape(boxes, comps)
            gate = gates_ref[first + place]
            for half in range(comps // 128):
                lanes = slice(half * 128, half * 128 + 128)
                left_ref[:, place * comps + half * 128 : place * comps + half * 128 + 128] = (
                    source[:, lanes] * gate
                )
        count = len(moves)
        operator = wide_ref[pl.ds(first, count)].reshape(count * comps, comps)
        total_ref[...] += jnp.dot(
            left_ref[:, : count * comps], operator, preferred_element_type=jnp.float32
        )

    def outer(index, carry):
        side, spot = index // 5, index % 5
        group(side * 4 - 2, spot - 2, side * 73 + spot * 5, (-2, -1, 0, 1, 2))
        return carry

    def edge(index, carry):
        level, side = index // 2, index % 2
        group(level - 1, side * 4 - 2, 25 + level * 16 + side * 11, (-2, -1, 0, 1, 2))
        return carry

    def inner(index, carry):
        level, spot = index // 3, index % 3
        group(level - 1, spot - 1, 30 + level * 16 + spot * 2, (-2, 2))
        return carry

    lax.fori_loop(0, 10, outer, 0)
    lax.fori_loop(0, 6, edge, 0)
    lax.fori_loop(0, 9, inner, 0)


def solution(mesh):
    return jax.shard_map(
        per_device,
        mesh=mesh,
        in_specs=(
            P(("rows", "bx", "by"), None),
            P(("rows", "bx", "by")),
            P(("rows", "bx", "by")),
            P(("rows", "bx", "by")),
            P("rows", "bx", "by", None),
            P(),
            P(),
            P(),
            P(),
        ),
        out_specs=(P("rows", "bx", "by", None), P(("rows", "bx", "by"))),
        check_vma=False,
    )
```

```python
import functools

import jax
import jax.numpy as jnp
from jax import lax
from jax.experimental import pallas as pl
from jax.experimental.pallas import tpu as pltpu
from jax.sharding import PartitionSpec as P

PAIR_CHUNK = 1024
VMEM = pl.BlockSpec(memory_space=pltpu.VMEM)


def offset_table():
    listed = []
    for shift_z in range(-2, 3):
        for shift_x in range(-2, 3):
            for shift_y in range(-2, 3):
                if max(abs(shift_z), abs(shift_x), abs(shift_y)) == 2:
                    listed.append((shift_z, shift_x, shift_y))
    return listed


def add_moments(mult_ref, dens_ref, live_ref, box_ref, near_ref):
    near = near_ref.shape[0]
    labels = lax.broadcasted_iota(jnp.int32, (near, PAIR_CHUNK), 0)
    near_ref[...] = jnp.zeros_like(near_ref)

    def step(index, carry):
        at = pl.ds(pl.multiple_of(index * PAIR_CHUNK, PAIR_CHUNK), PAIR_CHUNK)
        weight = dens_ref[:, at] * live_ref[:, at].astype(jnp.float32)
        selector = jnp.where(labels == box_ref[:, at], weight, 0.0).astype(jnp.bfloat16)
        near_ref[...] += jnp.dot(selector, mult_ref[at, :], preferred_element_type=jnp.float32)
        return carry

    lax.fori_loop(0, mult_ref.shape[0] // PAIR_CHUNK, step, 0)


def add_pairs(locals_ref, first, jump, mult_ref, box_ref, pairs_ref, fresh):
    count = locals_ref.shape[0]
    labels = lax.broadcasted_iota(jnp.int32, (count, PAIR_CHUNK), 0) + first
    if jump:
        labels = labels + jnp.where(labels >= count // 2, jump, 0)

    def step(index, carry):
        at = pl.ds(pl.multiple_of(index * PAIR_CHUNK, PAIR_CHUNK), PAIR_CHUNK)
        values = lax.dot_general(
            locals_ref[...],
            mult_ref[at, :],
            (((1,), (1,)), ((), ())),
            preferred_element_type=jnp.float32,
        )
        hits = jnp.where(labels == box_ref[:, at], values, 0.0)
        found = jnp.sum(hits, 0, keepdims=True)
        pairs_ref[:, at] = found if fresh else pairs_ref[:, at] + found
        return carry

    lax.fori_loop(0, mult_ref.shape[0] // PAIR_CHUNK, step, 0)


def neighbour(axis, move):
    count = lax.axis_size(axis)
    return {axis: lax.rem(lax.axis_index(axis) + (move + count), count)}


def send(source, target, sems, index, device):
    copy = pltpu.make_async_remote_copy(
        src_ref=source,
        dst_ref=target,
        send_sem=sems.at[0, index],
        recv_sem=sems.at[1, index],
        device_id=device,
        device_id_type=pl.DeviceIdType.MESH,
    )
    copy.start()
    return copy


def share_cells(axis, own_ref, slots_ref, sems):
    return [
        send(own_ref, slots_ref.at[move - 1], sems, move - 1, neighbour(axis, move))
        for move in range(1, lax.axis_size(axis))
    ]


def collect_cells(copies, own_ref, slots_ref):
    value = own_ref[...]
    for place, copy in enumerate(copies):
        copy.wait_recv()
        value = value + slots_ref[place]
    return value


def fused_kernel(
    sizes, mult_ref, dens_ref, live_ref, box_ref, mask_ref, rows_ref, cols_ref, base_ref, lattice_ref,
    out_ref, pairs_ref,
    near_ref, zsend_ref, zrecv_ref, full_ref, padded_ref, pack_ref, ysend_ref, yrecv_ref, lrecv_ref,
    cells_ref, cells_r, cells_x, cells_y, gates_ref, wide_ref, shifted_ref, total_ref, rows_pad, turned_ref,
    zsem, xsem, ysem, lsem, crsem, cxsem, cysem,
):
    size_z, size_x, size_y = sizes
    plane = size_x * size_y
    near_z, near_x = size_z + 4, size_x + 4
    comps = near_ref.shape[1]
    axes = ("rows", "bx", "by")
    barrier = pltpu.get_barrier_semaphore()
    peers = 0
    for axis in axes:
        for move in range(1, lax.axis_size(axis)):
            pl.semaphore_signal(
                barrier, inc=1, device_id=neighbour(axis, move), device_id_type=pl.DeviceIdType.MESH
            )
            peers += 1

    add_moments(mult_ref, dens_ref, live_ref, box_ref, near_ref)
    zsend_ref[0] = near_ref[: 4 * plane].astype(jnp.bfloat16)
    zsend_ref[1] = near_ref[size_z * plane :].astype(jnp.bfloat16)
    pl.semaphore_wait(barrier, peers)
    waits = [
        send(zsend_ref.at[0], zrecv_ref.at[1], zsem, 0, neighbour("rows", -1)),
        send(zsend_ref.at[1], zrecv_ref.at[0], zsem, 1, neighbour("rows", 1)),
    ]
    zcopies = list(waits)
    cells_ref[0] = jnp.broadcast_to(jnp.sum(near_ref[...], 0, keepdims=True), (8, comps))
    rcopies = share_cells("rows", cells_ref.at[0], cells_r, crsem)
    waits += rcopies

    rows_pad[...] = jnp.zeros_like(rows_pad)
    rows_pad[: rows_ref.shape[0], :] = rows_ref[...]
    turned_ref[...] = rows_pad[...].T
    expand_operators(turned_ref, cols_ref, base_ref, wide_ref)
    expand_masks(mask_ref, gates_ref, 0, 1)

    for copy in zcopies:
        copy.wait_recv()
    near_ref[: 4 * plane] += zrecv_ref[0].astype(jnp.float32)
    near_ref[size_z * plane :] += zrecv_ref[1].astype(jnp.float32)
    own = pl.ds(2 * size_y, plane)
    for level in range(near_z):
        full_ref[level, own, :] = near_ref[level * plane : (level + 1) * plane].astype(jnp.bfloat16)
    edge = 2 * size_y
    xcopies = [
        send(
            full_ref.at[:, pl.ds(edge, edge), :], full_ref.at[:, pl.ds(edge + plane, edge), :],
            xsem, 0, neighbour("bx", -1),
        ),
        send(
            full_ref.at[:, pl.ds(plane, edge), :], full_ref.at[:, pl.ds(0, edge), :],
            xsem, 1, neighbour("bx", 1),
        ),
    ]
    waits += xcopies
    cells_ref[1] = collect_cells(rcopies, cells_ref.at[0], cells_r)
    bcopies = share_cells("bx", cells_ref.at[1], cells_x, cxsem)
    waits += bcopies

    expand_masks(mask_ref, gates_ref, 1, 2)

    for copy in xcopies:
        copy.wait_recv()

    def pack(level, carry):
        values = full_ref[level].astype(jnp.float32).reshape(near_x, size_y, comps)
        padded_ref[level, :, 2 : 2 + size_y, :] = values
        for x in range(near_x):
            pack_ref[0, level, 2 * x : 2 * x + 2, :] = values[x, :2, :]
            pack_ref[1, level, 2 * x : 2 * x + 2, :] = values[x, size_y - 2 :, :]
        return carry

    lax.fori_loop(0, near_z, pack, 0)
    ysend_ref[...] = pack_ref[...].reshape(ysend_ref.shape).astype(jnp.bfloat16)
    ycopies = [
        send(ysend_ref.at[0], yrecv_ref.at[1], ysem, 0, neighbour("by", -1)),
        send(ysend_ref.at[1], yrecv_ref.at[0], ysem, 1, neighbour("by", 1)),
    ]
    waits += ycopies
    cells_ref[2] = collect_cells(bcopies, cells_ref.at[1], cells_x)
    ccopies = share_cells("by", cells_ref.at[2], cells_y, cysem)
    waits += ccopies
    shifted_copies(padded_ref, shifted_ref, (2,))
    expand_masks(mask_ref, gates_ref, 2, 4)
    for copy in ycopies:
        copy.wait_recv()
    pack_ref[...] = yrecv_ref[...].astype(jnp.float32).reshape(pack_ref.shape)

    def unpack(level, carry):
        for x in range(near_x):
            padded_ref[level, x, :2, :] = pack_ref[0, level, 2 * x : 2 * x + 2, :]
            padded_ref[level, x, 2 + size_y :, :] = pack_ref[1, level, 2 * x : 2 * x + 2, :]
        return carry

    lax.fori_loop(0, near_z, unpack, 0)
    shifted_copies(padded_ref, shifted_ref, (0, 1, 3, 4))

    cell = collect_cells(ccopies, cells_ref.at[2], cells_y)
    term = jnp.dot(
        cell, lattice_ref[...], precision=lax.Precision.HIGHEST, preferred_element_type=jnp.float32
    )
    total_ref[...] = jnp.broadcast_to(term[:1], total_ref.shape)
    far_field(shifted_ref, gates_ref, wide_ref, total_ref, sizes)
    out_ref[...] = total_ref[...].astype(jnp.bfloat16)
    boxes = size_z * plane
    lcopies = [
        send(out_ref.at[pl.ds(0, 2 * plane)], lrecv_ref.at[pl.ds(2 * plane, 2 * plane)], lsem, 0, neighbour("rows", -1)),
        send(out_ref.at[pl.ds(boxes - 2 * plane, 2 * plane)], lrecv_ref.at[pl.ds(0, 2 * plane)], lsem, 1, neighbour("rows", 1)),
    ]
    waits += lcopies
    add_pairs(out_ref, 2 * plane, 0, mult_ref, box_ref, pairs_ref, True)
    for copy in lcopies:
        copy.wait_recv()
    add_pairs(lrecv_ref, 0, boxes, mult_ref, box_ref, pairs_ref, False)
    for copy in waits:
        copy.wait_send()


def per_device(
    pair_mult, pair_dens, pair_live, pair_box, inter_mask, row_scale, col_scale, base, lattice
):
    pairs, comps = pair_mult.shape
    depth, width_x, width_y, offsets = inter_mask.shape
    plane = width_x * width_y
    boxes = depth * plane
    near = boxes + 4 * plane
    edge_rows = (depth + 4) * (width_x + 4) * 2
    counts = [lax.axis_size(axis) - 1 for axis in ("rows", "bx", "by")]
    b16, f32 = jnp.bfloat16, jnp.float32
    box_locals, pair_j = pl.pallas_call(
        functools.partial(fused_kernel, (depth, width_x, width_y)),
        out_shape=(
            jax.ShapeDtypeStruct((boxes, comps), b16),
            jax.ShapeDtypeStruct((1, pairs), f32),
        ),
        in_specs=[VMEM] * 9,
        out_specs=(VMEM, VMEM),
        scratch_shapes=[
            pltpu.VMEM((near, comps), f32),
            pltpu.VMEM((2, 4 * plane, comps), b16),
            pltpu.VMEM((2, 4 * plane, comps), b16),
            pltpu.VMEM((depth + 4, (width_x + 4) * width_y, comps), b16),
            pltpu.VMEM((depth + 4, width_x + 4, width_y + 4, comps), f32),
            pltpu.VMEM((2, depth + 4, 2 * (width_x + 4), comps), f32),
            pltpu.VMEM((2, edge_rows, comps), b16),
            pltpu.VMEM((2, edge_rows, comps), b16),
            pltpu.VMEM((4 * plane, comps), b16),
            pltpu.VMEM((3, 8, comps), f32),
        ]
        + [pltpu.VMEM((count, 8, comps), f32) for count in counts]
        + [
            pltpu.VMEM((offsets, boxes, 128), b16),
            pltpu.VMEM((offsets, comps, comps), b16),
            pltpu.VMEM((5, 2, depth + 4, (width_x + 4) * width_y, comps), b16),
            pltpu.VMEM((boxes, comps), f32),
            pltpu.VMEM((128, comps), f32),
            pltpu.VMEM((comps, 128), f32),
        ]
        + [pltpu.SemaphoreType.DMA((2, 2))] * 4
        + [pltpu.SemaphoreType.DMA((2, count)) for count in counts],
        compiler_params=pltpu.CompilerParams(
            vmem_limit_bytes=56 * 1024 * 1024, collective_id=0, has_side_effects=True
        ),
    )(
        pair_mult, pair_dens.reshape(1, pairs), pair_live.reshape(1, pairs), pair_box.reshape(1, pairs),
        inter_mask.reshape(boxes, offsets), row_scale, col_scale, base, lattice,
    )
    return (box_locals.reshape(depth, width_x, width_y, comps), pair_j.reshape(pairs))


def expand_operators(rows_ref, cols_ref, base_ref, wide_ref):
    offsets, comps, outs = wide_ref.shape

    def step(index, carry):
        at = pl.ds(pl.multiple_of(index * 16, 16), 16)
        core = base_ref[at, :].astype(jnp.float32)
        rows = rows_ref[at, :].astype(jnp.bfloat16)
        for entry in range(offsets):
            scaled = (core * cols_ref[entry : entry + 1, :]).astype(jnp.bfloat16)
            wide_ref[entry, at, :] = scaled * rows[:, entry : entry + 1]
        return carry

    lax.fori_loop(0, comps // 16, step, 0)


def expand_masks(mask_ref, wide_ref, begin, end):
    offsets, boxes, lanes = wide_ref.shape

    def step(index, carry):
        at = pl.ds(pl.multiple_of(index * 32, 32), 32)
        gates = mask_ref[at, :].astype(jnp.float32)
        for entry in range(offsets):
            wide = jnp.broadcast_to(gates[:, entry : entry + 1], (32, lanes))
            wide_ref[entry, at, :] = wide.astype(jnp.bfloat16)
        return carry

    blocks = boxes // 32
    lax.fori_loop(blocks * begin // 4, blocks * end // 4, step, 0)


def shifted_copies(padded_ref, shifted_ref, moves):
    depth = padded_ref.shape[0]
    size_y = padded_ref.shape[2] - 4
    spread_x = padded_ref.shape[1]
    comps = padded_ref.shape[3]

    def step(level, carry):
        for move in moves:
            part = padded_ref[level, :, move : move + size_y, :].astype(jnp.bfloat16)
            shifted_ref[move, 0, level] = part.reshape(spread_x * size_y, comps)
            part = padded_ref[level, 1 : spread_x - 1, move : move + size_y, :].astype(jnp.bfloat16)
            shifted_ref[move, 1, level, : (spread_x - 2) * size_y] = part.reshape(
                (spread_x - 2) * size_y, comps
            )
        return carry

    lax.fori_loop(0, depth, step, 0)


def far_field(shifted_ref, gates_ref, wide_ref, total_ref, sizes):
    size_z, size_x, size_y = sizes
    rows = size_x * size_y
    boxes = size_z * rows
    comps = wide_ref.shape[1]

    def group(shift_z, shift_x, first, moves):
        even = (shift_x + 2) % 2
        start = pl.multiple_of(((shift_x + 2) // 2) * 2 * size_y, 2 * size_y)
        left = []
        for place, move in enumerate(moves):
            source = shifted_ref[move + 2, even, pl.ds(shift_z + 2, size_z), pl.ds(start, rows), :]
            source = source.reshape(boxes, comps)
            gate = gates_ref[first + place]
            for half in range(comps // 128):
                lanes = slice(half * 128, half * 128 + 128)
                left.append(source[:, lanes] * gate)
        count = len(moves)
        operator = wide_ref[pl.ds(first, count)].reshape(count * comps, comps)
        total_ref[...] += jnp.dot(
            jnp.concatenate(left, axis=1), operator, preferred_element_type=jnp.float32
        )

    def outer(index, carry):
        side, spot = index // 5, index % 5
        group(side * 4 - 2, spot - 2, side * 73 + spot * 5, (-2, -1, 0, 1, 2))
        return carry

    def edge(index, carry):
        level, side = index // 2, index % 2
        group(level - 1, side * 4 - 2, 25 + level * 16 + side * 11, (-2, -1, 0, 1, 2))
        return carry

    def inner(index, carry):
        level, spot = index // 3, index % 3
        group(level - 1, spot - 1, 30 + level * 16 + spot * 2, (-2, 2))
        return carry

    lax.fori_loop(0, 10, outer, 0)
    lax.fori_loop(0, 6, edge, 0)
    lax.fori_loop(0, 9, inner, 0)


def solution(mesh):
    return jax.shard_map(
        per_device,
        mesh=mesh,
        in_specs=(
            P(("rows", "bx", "by"), None),
            P(("rows", "bx", "by")),
            P(("rows", "bx", "by")),
            P(("rows", "bx", "by")),
            P("rows", "bx", "by", None),
            P(),
            P(),
            P(),
            P(),
        ),
        out_specs=(P("rows", "bx", "by", None), P(("rows", "bx", "by"))),
        check_vma=False,
    )
```

```python
import functools

import jax
import jax.numpy as jnp
from jax import lax
from jax.experimental import pallas as pl
from jax.experimental.pallas import tpu as pltpu
from jax.sharding import PartitionSpec as P

PAIR_CHUNK = 1024
VMEM = pl.BlockSpec(memory_space=pltpu.VMEM)


def offset_table():
    listed = []
    for shift_z in range(-2, 3):
        for shift_x in range(-2, 3):
            for shift_y in range(-2, 3):
                if max(abs(shift_z), abs(shift_x), abs(shift_y)) == 2:
                    listed.append((shift_z, shift_x, shift_y))
    return listed


def add_moments(mult_ref, dens_ref, live_ref, box_ref, near_ref, starts, length):
    labels = jnp.concatenate(
        [lax.broadcasted_iota(jnp.int32, (length, PAIR_CHUNK), 0) + start for start in starts], axis=0
    )
    for start in starts:
        near_ref[start : start + length, :] = jnp.zeros((length, near_ref.shape[1]), jnp.float32)

    def step(index, carry):
        at = pl.ds(pl.multiple_of(index * PAIR_CHUNK, PAIR_CHUNK), PAIR_CHUNK)
        weight = dens_ref[:, at] * live_ref[:, at].astype(jnp.float32)
        selector = jnp.where(labels == box_ref[:, at], weight, 0.0).astype(jnp.bfloat16)
        sums = jnp.dot(selector, mult_ref[at, :], preferred_element_type=jnp.float32)
        for place, start in enumerate(starts):
            near_ref[start : start + length, :] += sums[place * length : (place + 1) * length]
        return carry

    lax.fori_loop(0, mult_ref.shape[0] // PAIR_CHUNK, step, 0)


def add_pairs(locals_ref, first, jump, mult_ref, box_ref, pairs_ref, fresh):
    count = locals_ref.shape[0]
    labels = lax.broadcasted_iota(jnp.int32, (count, PAIR_CHUNK), 0) + first
    if jump:
        labels = labels + jnp.where(labels >= count // 2, jump, 0)

    def step(index, carry):
        at = pl.ds(pl.multiple_of(index * PAIR_CHUNK, PAIR_CHUNK), PAIR_CHUNK)
        values = lax.dot_general(
            locals_ref[...],
            mult_ref[at, :],
            (((1,), (1,)), ((), ())),
            preferred_element_type=jnp.float32,
        )
        hits = jnp.where(labels == box_ref[:, at], values, 0.0)
        found = jnp.sum(hits, 0, keepdims=True)
        pairs_ref[:, at] = found if fresh else pairs_ref[:, at] + found
        return carry

    lax.fori_loop(0, mult_ref.shape[0] // PAIR_CHUNK, step, 0)


def neighbour(axis, move):
    count = lax.axis_size(axis)
    return {axis: lax.rem(lax.axis_index(axis) + (move + count), count)}


def send(source, target, sems, index, device):
    copy = pltpu.make_async_remote_copy(
        src_ref=source,
        dst_ref=target,
        send_sem=sems.at[0, index],
        recv_sem=sems.at[1, index],
        device_id=device,
        device_id_type=pl.DeviceIdType.MESH,
    )
    copy.start()
    return copy


def share_cells(axis, own_ref, slots_ref, sems):
    return [
        send(own_ref, slots_ref.at[move - 1], sems, move - 1, neighbour(axis, move))
        for move in range(1, lax.axis_size(axis))
    ]


def collect_cells(copies, own_ref, slots_ref):
    value = own_ref[...]
    for place, copy in enumerate(copies):
        copy.wait_recv()
        value = value + slots_ref[place]
    return value


def fused_kernel(
    sizes, mult_ref, dens_ref, live_ref, box_ref, mask_ref, rows_ref, cols_ref, base_ref, lattice_ref,
    out_ref, pairs_ref,
    near_ref, zsend_ref, zrecv_ref, full_ref, padded_ref, pack_ref, ysend_ref, yrecv_ref, lrecv_ref,
    cells_ref, cells_r, cells_x, cells_y, gates_ref, wide_ref, shifted_ref, total_ref, rows_pad, turned_ref,
    zsem, xsem, ysem, lsem, crsem, cxsem, cysem,
):
    size_z, size_x, size_y = sizes
    plane = size_x * size_y
    near_z, near_x = size_z + 4, size_x + 4
    comps = near_ref.shape[1]
    axes = ("rows", "bx", "by")
    barrier = pltpu.get_barrier_semaphore()
    peers = 0
    for axis in axes:
        for move in range(1, lax.axis_size(axis)):
            pl.semaphore_signal(
                barrier, inc=1, device_id=neighbour(axis, move), device_id_type=pl.DeviceIdType.MESH
            )
            peers += 1

    pair_refs = (mult_ref, dens_ref, live_ref, box_ref, near_ref)
    add_moments(*pair_refs, (0, size_z * plane), 4 * plane)
    zsend_ref[0] = near_ref[: 4 * plane].astype(jnp.bfloat16)
    zsend_ref[1] = near_ref[size_z * plane :].astype(jnp.bfloat16)
    pl.semaphore_wait(barrier, peers)
    waits = [
        send(zsend_ref.at[0], zrecv_ref.at[1], zsem, 0, neighbour("rows", -1)),
        send(zsend_ref.at[1], zrecv_ref.at[0], zsem, 1, neighbour("rows", 1)),
    ]
    zcopies = list(waits)
    add_moments(*pair_refs, (4 * plane,), (size_z - 4) * plane)
    cells_ref[0] = jnp.broadcast_to(jnp.sum(near_ref[...], 0, keepdims=True), (8, comps))
    rcopies = share_cells("rows", cells_ref.at[0], cells_r, crsem)
    waits += rcopies

    rows_pad[...] = jnp.zeros_like(rows_pad)
    rows_pad[: rows_ref.shape[0], :] = rows_ref[...]
    turned_ref[...] = rows_pad[...].T
    expand_operators(turned_ref, cols_ref, base_ref, wide_ref)
    expand_masks(mask_ref, gates_ref, 0, 1)

    for copy in zcopies:
        copy.wait_recv()
    near_ref[: 4 * plane] += zrecv_ref[0].astype(jnp.float32)
    near_ref[size_z * plane :] += zrecv_ref[1].astype(jnp.float32)
    own = pl.ds(2 * size_y, plane)
    for level in range(near_z):
        full_ref[level, own, :] = near_ref[level * plane : (level + 1) * plane].astype(jnp.bfloat16)
    edge = 2 * size_y
    xcopies = [
        send(
            full_ref.at[:, pl.ds(edge, edge), :], full_ref.at[:, pl.ds(edge + plane, edge), :],
            xsem, 0, neighbour("bx", -1),
        ),
        send(
            full_ref.at[:, pl.ds(plane, edge), :], full_ref.at[:, pl.ds(0, edge), :],
            xsem, 1, neighbour("bx", 1),
        ),
    ]
    waits += xcopies
    cells_ref[1] = collect_cells(rcopies, cells_ref.at[0], cells_r)
    bcopies = share_cells("bx", cells_ref.at[1], cells_x, cxsem)
    waits += bcopies

    expand_masks(mask_ref, gates_ref, 1, 2)

    for copy in xcopies:
        copy.wait_recv()

    def pack(level, carry):
        values = full_ref[level].astype(jnp.float32).reshape(near_x, size_y, comps)
        padded_ref[level, :, 2 : 2 + size_y, :] = values
        for x in range(near_x):
            pack_ref[0, level, 2 * x : 2 * x + 2, :] = values[x, :2, :]
            pack_ref[1, level, 2 * x : 2 * x + 2, :] = values[x, size_y - 2 :, :]
        return carry

    lax.fori_loop(0, near_z, pack, 0)
    ysend_ref[...] = pack_ref[...].reshape(ysend_ref.shape).astype(jnp.bfloat16)
    ycopies = [
        send(ysend_ref.at[0], yrecv_ref.at[1], ysem, 0, neighbour("by", -1)),
        send(ysend_ref.at[1], yrecv_ref.at[0], ysem, 1, neighbour("by", 1)),
    ]
    waits += ycopies
    cells_ref[2] = collect_cells(bcopies, cells_ref.at[1], cells_x)
    ccopies = share_cells("by", cells_ref.at[2], cells_y, cysem)
    waits += ccopies
    shifted_copies(padded_ref, shifted_ref, (2,))
    expand_masks(mask_ref, gates_ref, 2, 4)
    total_ref[...] = jnp.zeros_like(total_ref)
    far_field(shifted_ref, gates_ref, wide_ref, total_ref, sizes, True)
    for copy in ycopies:
        copy.wait_recv()
    pack_ref[...] = yrecv_ref[...].astype(jnp.float32).reshape(pack_ref.shape)

    def unpack(level, carry):
        for x in range(near_x):
            padded_ref[level, x, :2, :] = pack_ref[0, level, 2 * x : 2 * x + 2, :]
            padded_ref[level, x, 2 + size_y :, :] = pack_ref[1, level, 2 * x : 2 * x + 2, :]
        return carry

    lax.fori_loop(0, near_z, unpack, 0)
    shifted_copies(padded_ref, shifted_ref, (0, 1, 3, 4))

    cell = collect_cells(ccopies, cells_ref.at[2], cells_y)
    term = jnp.dot(
        cell, lattice_ref[...], precision=lax.Precision.HIGHEST, preferred_element_type=jnp.float32
    )
    far_field(shifted_ref, gates_ref, wide_ref, total_ref, sizes, False)
    out_ref[...] = (total_ref[...] + term[:1]).astype(jnp.bfloat16)
    boxes = size_z * plane
    lcopies = [
        send(out_ref.at[pl.ds(0, 2 * plane)], lrecv_ref.at[pl.ds(2 * plane, 2 * plane)], lsem, 0, neighbour("rows", -1)),
        send(out_ref.at[pl.ds(boxes - 2 * plane, 2 * plane)], lrecv_ref.at[pl.ds(0, 2 * plane)], lsem, 1, neighbour("rows", 1)),
    ]
    waits += lcopies
    add_pairs(out_ref, 2 * plane, 0, mult_ref, box_ref, pairs_ref, True)
    for copy in lcopies:
        copy.wait_recv()
    add_pairs(lrecv_ref, 0, boxes, mult_ref, box_ref, pairs_ref, False)
    for copy in waits:
        copy.wait_send()


def per_device(
    pair_mult, pair_dens, pair_live, pair_box, inter_mask, row_scale, col_scale, base, lattice
):
    pairs, comps = pair_mult.shape
    depth, width_x, width_y, offsets = inter_mask.shape
    plane = width_x * width_y
    boxes = depth * plane
    near = boxes + 4 * plane
    edge_rows = (depth + 4) * (width_x + 4) * 2
    counts = [lax.axis_size(axis) - 1 for axis in ("rows", "bx", "by")]
    b16, f32 = jnp.bfloat16, jnp.float32
    box_locals, pair_j = pl.pallas_call(
        functools.partial(fused_kernel, (depth, width_x, width_y)),
        out_shape=(
            jax.ShapeDtypeStruct((boxes, comps), b16),
            jax.ShapeDtypeStruct((1, pairs), f32),
        ),
        in_specs=[VMEM] * 9,
        out_specs=(VMEM, VMEM),
        scratch_shapes=[
            pltpu.VMEM((near, comps), f32),
            pltpu.VMEM((2, 4 * plane, comps), b16),
            pltpu.VMEM((2, 4 * plane, comps), b16),
            pltpu.VMEM((depth + 4, (width_x + 4) * width_y, comps), b16),
            pltpu.VMEM((depth + 4, width_x + 4, width_y + 4, comps), f32),
            pltpu.VMEM((2, depth + 4, 2 * (width_x + 4), comps), f32),
            pltpu.VMEM((2, edge_rows, comps), b16),
            pltpu.VMEM((2, edge_rows, comps), b16),
            pltpu.VMEM((4 * plane, comps), b16),
            pltpu.VMEM((3, 8, comps), f32),
        ]
        + [pltpu.VMEM((count, 8, comps), f32) for count in counts]
        + [
            pltpu.VMEM((offsets, boxes, 128), b16),
            pltpu.VMEM((offsets, comps, comps), b16),
            pltpu.VMEM((5, 2, depth + 4, (width_x + 4) * width_y, comps), b16),
            pltpu.VMEM((boxes, comps), f32),
            pltpu.VMEM((128, comps), f32),
            pltpu.VMEM((comps, 128), f32),
        ]
        + [pltpu.SemaphoreType.DMA((2, 2))] * 4
        + [pltpu.SemaphoreType.DMA((2, count)) for count in counts],
        compiler_params=pltpu.CompilerParams(
            vmem_limit_bytes=56 * 1024 * 1024, collective_id=0, has_side_effects=True
        ),
    )(
        pair_mult, pair_dens.reshape(1, pairs), pair_live.reshape(1, pairs), pair_box.reshape(1, pairs),
        inter_mask.reshape(boxes, offsets), row_scale, col_scale, base, lattice,
    )
    return (box_locals.reshape(depth, width_x, width_y, comps), pair_j.reshape(pairs))


def expand_operators(rows_ref, cols_ref, base_ref, wide_ref):
    offsets, comps, outs = wide_ref.shape

    def step(index, carry):
        at = pl.ds(pl.multiple_of(index * 16, 16), 16)
        core = base_ref[at, :].astype(jnp.float32)
        rows = rows_ref[at, :].astype(jnp.bfloat16)
        for entry in range(offsets):
            scaled = (core * cols_ref[entry : entry + 1, :]).astype(jnp.bfloat16)
            wide_ref[entry, at, :] = scaled * rows[:, entry : entry + 1]
        return carry

    lax.fori_loop(0, comps // 16, step, 0)


def expand_masks(mask_ref, wide_ref, begin, end):
    offsets, boxes, lanes = wide_ref.shape

    def step(index, carry):
        at = pl.ds(pl.multiple_of(index * 32, 32), 32)
        gates = mask_ref[at, :].astype(jnp.float32)
        for entry in range(offsets):
            wide = jnp.broadcast_to(gates[:, entry : entry + 1], (32, lanes))
            wide_ref[entry, at, :] = wide.astype(jnp.bfloat16)
        return carry

    blocks = boxes // 32
    lax.fori_loop(blocks * begin // 4, blocks * end // 4, step, 0)


def shifted_copies(padded_ref, shifted_ref, moves):
    depth = padded_ref.shape[0]
    size_y = padded_ref.shape[2] - 4
    spread_x = padded_ref.shape[1]
    comps = padded_ref.shape[3]

    def step(level, carry):
        for move in moves:
            part = padded_ref[level, :, move : move + size_y, :].astype(jnp.bfloat16)
            shifted_ref[move, 0, level] = part.reshape(spread_x * size_y, comps)
            part = padded_ref[level, 1 : spread_x - 1, move : move + size_y, :].astype(jnp.bfloat16)
            shifted_ref[move, 1, level, : (spread_x - 2) * size_y] = part.reshape(
                (spread_x - 2) * size_y, comps
            )
        return carry

    lax.fori_loop(0, depth, step, 0)


def far_field(shifted_ref, gates_ref, wide_ref, total_ref, sizes, central):
    size_z, size_x, size_y = sizes
    rows = size_x * size_y
    boxes = size_z * rows
    comps = wide_ref.shape[1]

    def group(shift_z, shift_x, first, pairs):
        even = (shift_x + 2) % 2
        start = pl.multiple_of(((shift_x + 2) // 2) * 2 * size_y, 2 * size_y)
        total = total_ref[...]
        for place, move in pairs:
            source = shifted_ref[move + 2, even, pl.ds(shift_z + 2, size_z), pl.ds(start, rows), :]
            source = source.reshape(boxes, comps)
            gate = gates_ref[first + place]
            left = [source[:, at : at + 128] * gate for at in range(0, comps, 128)]
            total = total + jnp.dot(
                jnp.concatenate(left, axis=1),
                wide_ref[first + place],
                preferred_element_type=jnp.float32,
            )
        total_ref[...] = total

    ring_moves = ((2, 0),) if central else ((0, -2), (1, -1), (3, 1), (4, 2))

    def outer(index, carry):
        side, spot = index // 5, index % 5
        group(side * 4 - 2, spot - 2, side * 73 + spot * 5, ring_moves)
        return carry

    def edge(index, carry):
        level, side = index // 2, index % 2
        group(level - 1, side * 4 - 2, 25 + level * 16 + side * 11, ring_moves)
        return carry

    def inner(index, carry):
        level, spot = index // 3, index % 3
        group(level - 1, spot - 1, 30 + level * 16 + spot * 2, ((0, -2), (1, 2)))
        return carry

    lax.fori_loop(0, 10, outer, 0)
    lax.fori_loop(0, 6, edge, 0)
    if not central:
        lax.fori_loop(0, 9, inner, 0)


def solution(mesh):
    return jax.shard_map(
        per_device,
        mesh=mesh,
        in_specs=(
            P(("rows", "bx", "by"), None),
            P(("rows", "bx", "by")),
            P(("rows", "bx", "by")),
            P(("rows", "bx", "by")),
            P("rows", "bx", "by", None),
            P(),
            P(),
            P(),
            P(),
        ),
        out_specs=(P("rows", "bx", "by", None), P(("rows", "bx", "by"))),
        check_vma=False,
    )
```
